32 devices in a mesh: shard: 8 (over y, x, core), grp: 4 (over z).
Axes of the slice: x: 2, y: 2, z: 4, core: 2. Of those that a mesh axis runs over, the one named last changes fastest.
Arguments:
- embeddings: float32 [16384, 1024], P(('shard', 'grp')), may hold values from -6 to 6
- cluster: int32 [16384, 1], P(('shard', 'grp')), may hold values from 0 to 7; in each aligned block of 512 rows (0 to 511, 512 to 1023, ...) at most 128 rows name the same one
Outputs:
- duplicate: float32 [16384], P(('shard', 'grp'))
- neighbour: float32 [16384, 1024], P(('shard', 'grp'))
The draws below stay inside these ranges and needn't reach their ends.
Inputs may be any that keep to these rules, and one draw needn't show every extreme that they name: Among the pages of one device, at most 128 belong to any one cluster.
All inputs are finite; a program needn't handle non-finite values.
Results may differ from the reference program's by a relative error of at most 0.0075.
Values may be sent and summed in bfloat16 or wider, within the bound.
No kernel may reach another device: no remote copies, remote signals or barrier semaphores. Data moves between devices by JAX's collectives and lax.ppermute only.
A program may use at most 128 MiB of HBM per device.

```python
import math
import jax
import jax.numpy as jnp
import numpy as np
from jax import lax

D = 1024
PAGES_DEV = 512
SLOT = 128
NCL = 8
CAP = 4096
PAGES = 16384


def levels(key, extent, cuts, least, top_value):
    def one(axis_at, blocks):
        steps = jax.random.uniform(jax.random.fold_in(jax.random.fold_in(key, 6), axis_at), (blocks,), jnp.float32, least / len(cuts), top_value / len(cuts))
        return jnp.repeat(jnp.exp(steps), extent[axis_at] // blocks).reshape((-1,) + (1,) * (len(extent) - axis_at - 1))

    factor_of = one(*cuts[0])
    for cut in cuts[1:]:
        factor_of = factor_of * one(*cut)
    return factor_of


def routed_block(rng, own, number, rows, count, top, limit, slope):
    sequence = jax.random.permutation(rng, count)
    heavy_load, usual = load_shares(count, rows * top, limit, slope, True), load_shares(count, rows * top, limit, slope, False)
    places = jnp.arange(count)

    def named(lengths, offset_by):
        used = int((lengths > 0).sum())
        fixed = max(1, used // 4)
        moved = fixed + (places - fixed + offset_by * (used - fixed)) % max(1, count - fixed)
        return jnp.zeros((count,), jnp.int32).at[sequence[jnp.where(places < fixed, places, moved)]].set(jnp.asarray(lengths, jnp.int32))

    lengths = jnp.where(number % 4 == 0, named(heavy_load, number // 4), named(usual, number - number // 4 - 1))
    mixed = jax.random.permutation(jax.random.fold_in(own, 3), count)
    donor, sink = mixed[0:count // 2 * 2:2], mixed[1:count // 2 * 2:2]
    room = jnp.minimum(lengths[donor] - 1, limit - lengths[sink]) // 2
    room = jnp.where((donor == sequence[0]) | (sink == sequence[0]) | (lengths[sink] == 0), 0, jnp.maximum(room, 0))
    moved = jax.random.randint(jax.random.fold_in(own, 4), (count // 2,), 0, 1 << 20) % (room + 1)
    lengths = lengths.at[donor].add(-moved).at[sink].add(moved)
    labels = jnp.searchsorted(jnp.cumsum(lengths), jnp.arange(rows * top), side="right").astype(jnp.int32)
    listing = labels.reshape(top, rows).T
    listing = listing[jax.random.permutation(jax.random.fold_in(own, 1), rows)]
    offset_by = jax.random.randint(jax.random.fold_in(own, 2), (rows, 1), 0, top)
    return jnp.take_along_axis(listing, (jnp.arange(top)[None, :] + offset_by) % top, axis=1)


def load_shares(number_of, total, reach, slope, full):
    portions = [(1 << 20) // math.isqrt(grade ** slope) + 1 for grade in range(1, number_of + 1)]
    largest = reach if full else min(reach, max(-(-total // number_of), total * portions[0] // sum(portions)))
    least = 1 if total - largest >= number_of - 1 else 0
    given, spare = [largest] + [least] * (number_of - 1), total - largest - least * (number_of - 1)
    while spare > 0:
        free = [i for i in range(1, number_of) if given[i] < largest] or [i for i in range(1, number_of) if given[i] < reach]
        mass, remaining = sum([portions[i] for i in free]), spare
        for i in free:
            extra = min(reach - given[i], max(1, remaining * portions[i] // mass), spare)
            given[i] = given[i] + extra
            spare = spare - extra
    return np.array(given)


def noise(rng, extent, scale, bound, shards=(), held_as=jnp.bfloat16):
    entries = scale * jax.random.normal(rng, extent, jnp.float32)
    if shards:
        entries = entries * levels(rng, extent, shards, -0.22, 0.18)
    return jnp.clip(entries, -bound, bound).astype(held_as)


def setup_inputs(seed: int = 0) -> dict:
    streams_of = jax.random.split(jax.random.key(seed), 3)
    embeddings = noise(streams_of[0], (PAGES, D), 1.0, 6.0, ((0, 32),), jnp.float32)
    cluster_keys = jax.random.split(jax.random.fold_in(streams_of[1], 1), PAGES // PAGES_DEV)
    cluster_turns = jax.random.permutation(jax.random.fold_in(streams_of[1], 3), PAGES // PAGES_DEV)
    cluster = jax.vmap(lambda own, number: routed_block(jax.random.fold_in(streams_of[1], 2), own, number, PAGES_DEV, NCL, 1, SLOT, 2))(cluster_keys, cluster_turns).reshape((PAGES, 1))
    return dict(embeddings=embeddings, cluster=cluster)


def normalize(embeddings):
    scale = lax.rsqrt(lax.optimization_barrier(jnp.mean(embeddings * embeddings, axis=1, keepdims=True)) + 1e-06)
    return (embeddings * scale).astype(jnp.bfloat16)

def reference(embeddings, cluster):
    npages = embeddings.shape[0]
    width = embeddings.shape[1]
    units = normalize(embeddings)
    ids = cluster[:, 0].astype(jnp.int32)
    onehot = (ids[:, None] == jnp.arange(NCL, dtype=jnp.int32)[None, :]).astype(jnp.int32)
    rank = (lax.optimization_barrier(jnp.sum(jnp.cumsum(onehot, axis=0) * onehot, axis=1)) - 1).astype(jnp.int32)
    members = jnp.zeros((NCL, CAP), jnp.int32).at[ids, rank].set(jnp.arange(npages, dtype=jnp.int32))
    live = jnp.zeros((NCL, CAP), jnp.float32).at[ids, rank].set(1.0)
    others = 1.0 - jnp.eye(CAP, dtype=jnp.float32)

    def per_cluster(packed):
        index, valid = packed
        rows = units[index]
        scores = jnp.dot(rows, rows.T, preferred_element_type=jnp.float32) * (64.0 / width)
        weight = jnp.exp(scores) * valid[None, :] * others
        count = lax.optimization_barrier(jnp.sum(weight, axis=1))
        pull = jnp.dot(weight.astype(jnp.bfloat16), rows, preferred_element_type=jnp.float32)
        return (jnp.log1p(count), pull / (1.0 + count)[:, None])
    dups, pulls = lax.map(per_cluster, (members, live))
    return (dups[ids, rank], pulls[ids, rank])
```

```python
import functools

import jax
import jax.numpy as jnp
from jax import lax
from jax.experimental import pallas as pl
from jax.experimental.pallas import tpu as pltpu
from jax.sharding import PartitionSpec as P

AXES = ("shard", "grp")
EXTRA = 8
MIB = 1 << 20


def hop_order(ng):
    return sorted(range(ng), key=lambda d: (min(d, ng - d), d))


def pack_kernel(hi_n, ng, slots, emb_ref, ids_ref, pos_ref, *out_refs):
    n, width = emb_ref.shape
    nb = hi_n * ng
    emb = emb_ref[...]
    scale = lax.rsqrt(jnp.mean(emb * emb, axis=1, keepdims=True) + 1e-06)
    units = (emb * scale).astype(jnp.bfloat16)
    hi = lax.axis_index("shard") // ng
    z = lax.axis_index("grp")
    ids = ids_ref[...]
    blk = jnp.zeros((1, n), jnp.int32)
    for k, dz in enumerate(hop_order(ng)):
        for dh in range(hi_n):
            owner = lax.rem(hi + dh, hi_n) * ng + lax.rem(z + dz, ng)
            blk = jnp.where(ids == owner, k * hi_n + dh, blk)
    onehot = lax.broadcasted_iota(jnp.int32, (nb, n), 0) == blk
    upto = lax.broadcasted_iota(jnp.int32, (n, n), 0) <= lax.broadcasted_iota(jnp.int32, (n, n), 1)
    cum = jnp.dot(
        onehot.astype(jnp.bfloat16), upto.astype(jnp.bfloat16), preferred_element_type=jnp.float32
    )
    rank = jnp.sum(jnp.where(onehot, cum, 0.0), axis=0, keepdims=True).astype(jnp.int32) - 1
    pos = blk * slots + rank
    pos_ref[...] = pos
    mark = float(2.0 * width**0.5)
    for k in range(nb):
        pick = lax.broadcasted_iota(jnp.int32, (slots, n), 0) + k * slots == pos
        rows = jnp.dot(pick.astype(jnp.bfloat16), units, preferred_element_type=jnp.float32)
        used = cum[k : k + 1, n - 1 : n].astype(jnp.int32)
        empty = lax.broadcasted_iota(jnp.int32, (slots, width), 0) >= used
        first = lax.broadcasted_iota(jnp.int32, (slots, width), 1) == 0
        out_refs[k][...] = jnp.where(empty & first, mark, rows).astype(jnp.bfloat16)


def weigh_kernel(sizes, blocks, own, slots, chunk, *refs):
    ncol = len(sizes)
    cols, outs = refs[:ncol], refs[ncol : ncol + len(blocks)]
    units, rows, pull, count, sems = refs[ncol + len(blocks) :]
    total, width = units.shape
    nrows = len(blocks) * slots
    starts = [sum(sizes[:i]) for i in range(ncol)]
    copies = [
        pltpu.make_async_copy(cols[i], units.at[pl.ds(starts[i], sizes[i])], sems.at[i])
        for i in range(ncol)
    ]
    for c in copies:
        c.start()
    waited = 0
    limit = 1.5 * width**0.5
    probe = lax.broadcasted_iota(jnp.int32, (16, width), 1) == 0
    rows[pl.ds(nrows, 16), :] = probe.astype(jnp.bfloat16)
    for at in range(0, total, chunk):
        need = own if at == 0 else at + chunk
        while waited < ncol and starts[waited] < need:
            copies[waited].wait()
            waited += 1
        if at == 0:
            for i, b in enumerate(blocks):
                rows[pl.ds(i * slots, slots), :] = units[pl.ds(b * slots, slots), :]
        part = units[pl.ds(at, chunk), :]
        scores = lax.dot_general(
            rows[...], part, (((1,), (1,)), ((), ())), preferred_element_type=jnp.float32
        )
        keep = jnp.broadcast_to(scores[nrows : nrows + 1, :] < limit, (nrows, chunk))
        if at < own:
            col = lax.broadcasted_iota(jnp.int32, (slots, chunk), 1) + at
            row = lax.broadcasted_iota(jnp.int32, (slots, chunk), 0)
            off = jnp.concatenate([col != row + b * slots for b in blocks], axis=0)
            keep = keep & off
        weight = jnp.where(keep, jnp.exp(scores[:nrows] * (64.0 / width)), 0.0)
        add_count = jnp.sum(weight, axis=1, keepdims=True)
        add_pull = jnp.dot(weight.astype(jnp.bfloat16), part, preferred_element_type=jnp.float32)
        if at == 0:
            count[...] = jnp.broadcast_to(add_count, count.shape)
            pull[...] = add_pull
        else:
            count[...] += jnp.broadcast_to(add_count, count.shape)
            pull[...] += add_pull
    valid = rows[pl.ds(0, nrows), 0:128].astype(jnp.float32)[:, 0:1] < limit
    for i in range(len(blocks)):
        at = i * slots
        ok = valid[at : at + slots]
        cnt = count[pl.ds(at, slots), :]
        near = pull[pl.ds(at, slots), :] / (1.0 + cnt[:, 0:1])
        outs[i][pl.ds(0, slots), :] = jnp.where(ok, near, 0.0).astype(jnp.bfloat16)
        dup = jnp.where(ok, jnp.log1p(cnt), 0.0)
        if slots < 128:
            dup = jnp.concatenate([dup, jnp.zeros((128 - slots, 128), jnp.float32)], axis=0)
        dup = dup.T[0:EXTRA]
        high = dup.astype(jnp.bfloat16).astype(jnp.float32)
        line = lax.broadcasted_iota(jnp.int32, (EXTRA, 128), 0)
        two = jnp.where(line == 0, high, jnp.where(line == 1, dup - high, 0.0))
        outs[i][pl.ds(slots, EXTRA), pl.ds(0, 128)] = two.astype(jnp.bfloat16)


def unpack_kernel(slots, pos_ref, *refs):
    blocks, dup_ref, near_ref = refs[:-2], refs[-2], refs[-1]
    n = pos_ref.shape[1]
    pos = pos_ref[...]
    dup = jnp.zeros((EXTRA, n), jnp.float32)
    for k, ref in enumerate(blocks):
        pick = lax.broadcasted_iota(jnp.int32, (slots, n), 0) + k * slots == pos
        pick = pick.astype(jnp.bfloat16)
        near = lax.dot_general(
            pick,
            ref[pl.ds(0, slots), :],
            (((0,), (0,)), ((), ())),
            preferred_element_type=jnp.float32,
        )
        if k == 0:
            near_ref[...] = near
        else:
            near_ref[...] += near
        two = ref[pl.ds(slots, EXTRA), pl.ds(0, 128)][:, :slots]
        dup = dup + jnp.dot(two, pick, preferred_element_type=jnp.float32)
    dup_ref[...] = dup[0:1] + dup[1:2]


def after(value, *deps):
    return lax.optimization_barrier((value,) + deps)[0]


def local(embeddings, cluster):
    n, width = embeddings.shape
    ns, ng = lax.axis_size("shard"), lax.axis_size("grp")
    hi_n = ns // ng
    nb = ns
    slots = 2 * n // ns
    own = nb * slots

    def moved(f):
        return [(s * ng + z, f(s, z)) for s in range(ns) for z in range(ng)]

    def to_owner(dh, dz, sign):
        return moved(
            lambda s, z: ((s // ng + sign * dh) % hi_n * ng + s % ng) * ng + (z + sign * dz) % ng
        )

    def beside(bit):
        return moved(lambda s, z: (s ^ bit) * ng + z)

    hops = [(dh, dz) for dz in hop_order(ng) for dh in range(hi_n)]
    vmem = pl.BlockSpec(memory_space=pltpu.VMEM)
    anyspace = pl.BlockSpec(memory_space=pl.ANY)
    ids = cluster.reshape(1, n)
    pos, *outbox = pl.pallas_call(
        functools.partial(pack_kernel, hi_n, ng, slots),
        out_shape=[jax.ShapeDtypeStruct((1, n), jnp.int32)]
        + [jax.ShapeDtypeStruct((slots, width), jnp.bfloat16)] * nb,
        in_specs=[vmem, vmem],
        out_specs=[vmem] * (nb + 1),
        compiler_params=pltpu.CompilerParams(vmem_limit_bytes=40 * MIB),
        name="pack",
    )(embeddings, ids)

    window = 3
    inbox = [outbox[0]]
    for k in range(1, nb):
        src = outbox[k]
        if k > window:
            src = after(src, inbox[k - window])
        inbox.append(lax.ppermute(src, AXES, to_owner(*hops[k], 1)))
    per = max(1, nb // 8)
    groups = [inbox[i : i + per] for i in range(0, nb, per)]
    near_by = [g[0] if len(g) == 1 else jnp.concatenate(g, axis=0) for g in groups]
    beyond = [lax.ppermute(g, AXES, beside(2)) for g in near_by]
    other = []
    for i in range(0, len(groups), 2):
        both = jnp.concatenate(near_by[i : i + 2] + beyond[i : i + 2], axis=0)
        other.append(lax.ppermute(both, AXES, beside(1)))
    columns = inbox + beyond + other
    sizes = [c.shape[0] for c in columns]
    total = sum(sizes)

    def weigh(blocks):
        nrows = len(blocks) * slots
        return pl.pallas_call(
            functools.partial(weigh_kernel, sizes, blocks, own, slots, 512),
            out_shape=[jax.ShapeDtypeStruct((slots + EXTRA, width), jnp.bfloat16)] * len(blocks),
            in_specs=[anyspace] * len(columns),
            out_specs=[vmem] * len(blocks),
            scratch_shapes=[
                pltpu.VMEM((total, width), jnp.bfloat16),
                pltpu.VMEM((nrows + 16, width), jnp.bfloat16),
                pltpu.VMEM((nrows, width), jnp.float32),
                pltpu.VMEM((nrows, 128), jnp.float32),
                pltpu.SemaphoreType.DMA((len(columns),)),
            ],
            compiler_params=pltpu.CompilerParams(vmem_limit_bytes=48 * MIB),
            cost_estimate=pl.CostEstimate(
                flops=4 * nrows * total * width,
                bytes_accessed=2 * total * width,
                transcendentals=nrows * total,
            ),
            name="weigh",
        )(*columns)

    result = [None] * nb
    far = list(range(nb - nb // 4, nb))
    rest = list(range(nb // 4, nb - nb // 4)) + list(range(nb // 4))
    for part in (far, rest):
        for b, r in zip(part, weigh(part)):
            result[b] = r
    back = [result[0]] + [None] * (nb - 1)
    for b in far + rest:
        if b:
            back[b] = lax.ppermute(result[b], AXES, to_owner(*hops[b], -1))
    dup, near = pl.pallas_call(
        functools.partial(unpack_kernel, slots),
        out_shape=[
            jax.ShapeDtypeStruct((1, n), jnp.float32),
            jax.ShapeDtypeStruct((n, width), jnp.float32),
        ],
        in_specs=[vmem] * (nb + 1),
        out_specs=[vmem, vmem],
        compiler_params=pltpu.CompilerParams(vmem_limit_bytes=40 * MIB),
        name="unpack",
    )(pos, *back)
    return dup.reshape(n), near


def solution(mesh):
    return jax.shard_map(
        local,
        mesh=mesh,
        in_specs=(P(("shard", "grp"), None), P(("shard", "grp"), None)),
        out_specs=(P(("shard", "grp")), P(("shard", "grp"), None)),
        check_vma=False,
    )
```

```python
import functools

import jax
import jax.numpy as jnp
from jax import lax
from jax.experimental import pallas as pl
from jax.experimental.pallas import tpu as pltpu
from jax.sharding import PartitionSpec as P

AXES = ("shard", "grp")
EXTRA = 8
MIB = 1 << 20


def hop_order(ng):
    return sorted(range(ng), key=lambda d: (min(d, ng - d), d))


def pack_kernel(hi_n, ng, slots, emb_ref, ids_ref, pos_ref, *out_refs):
    n, width = emb_ref.shape
    nb = hi_n * ng
    emb = emb_ref[...]
    scale = lax.rsqrt(jnp.mean(emb * emb, axis=1, keepdims=True) + 1e-06)
    units = (emb * scale).astype(jnp.bfloat16)
    hi = lax.axis_index("shard") // ng
    z = lax.axis_index("grp")
    ids = ids_ref[...]
    blk = jnp.zeros((1, n), jnp.int32)
    for k, dz in enumerate(hop_order(ng)):
        for dh in range(hi_n):
            owner = lax.rem(hi + dh, hi_n) * ng + lax.rem(z + dz, ng)
            blk = jnp.where(ids == owner, k * hi_n + dh, blk)
    onehot = lax.broadcasted_iota(jnp.int32, (nb, n), 0) == blk
    upto = lax.broadcasted_iota(jnp.int32, (n, n), 0) <= lax.broadcasted_iota(jnp.int32, (n, n), 1)
    cum = jnp.dot(
        onehot.astype(jnp.bfloat16), upto.astype(jnp.bfloat16), preferred_element_type=jnp.float32
    )
    rank = jnp.sum(jnp.where(onehot, cum, 0.0), axis=0, keepdims=True).astype(jnp.int32) - 1
    pos = blk * slots + rank
    pos_ref[...] = pos
    mark = float(2.0 * width**0.5)
    for k in range(nb):
        pick = lax.broadcasted_iota(jnp.int32, (slots, n), 0) + k * slots == pos
        rows = jnp.dot(pick.astype(jnp.bfloat16), units, preferred_element_type=jnp.float32)
        used = cum[k : k + 1, n - 1 : n].astype(jnp.int32)
        empty = lax.broadcasted_iota(jnp.int32, (slots, width), 0) >= used
        first = lax.broadcasted_iota(jnp.int32, (slots, width), 1) == 0
        out_refs[k][...] = jnp.where(empty & first, mark, rows).astype(jnp.bfloat16)


def weigh_kernel(layout, row_stage, slots, nblocks, carried, last, *refs):
    sizes = [n for _, ns in layout for n in ns]
    ncol, nunit = len(sizes), len(row_stage)
    refs = list(refs)
    row_in, cols = refs[:nunit], refs[nunit : nunit + ncol]
    del refs[: nunit + ncol]
    if carried:
        pull_in, count_in = refs[:2]
        del refs[:2]
    if last:
        outs = refs[:nblocks]
        del refs[:nblocks]
        units, rows, pull, count, sems = refs
    else:
        pull, count, units, rows, sems = refs
    total, width = units.shape
    unit = row_in[0].shape[0]
    nrows = nunit * unit
    starts = [sum(sizes[:i]) for i in range(ncol)]
    copies = [
        pltpu.make_async_copy(row_in[i], rows.at[pl.ds(i * unit, unit)], sems.at[i])
        for i in range(nunit)
    ]
    copies += [
        pltpu.make_async_copy(cols[i], units.at[pl.ds(starts[i], sizes[i])], sems.at[nunit + i])
        for i in range(ncol)
    ]
    for c in copies:
        c.start()
    limit = 1.5 * width**0.5
    probe = lax.broadcasted_iota(jnp.int32, (16, width), 1) == 0
    rows[pl.ds(nrows, 16), :] = probe.astype(jnp.bfloat16)
    for c in copies[:nunit]:
        c.wait()
    waited = 0
    at = 0
    for stage, ns in layout:
        size = sum(ns)
        chunk = min(size, 4 * unit)
        for half in range(size // chunk):
            while waited < ncol and starts[waited] < at + chunk:
                copies[nunit + waited].wait()
                waited += 1
            part = units[pl.ds(at, chunk), :]
            scores = lax.dot_general(
                rows[...], part, (((1,), (1,)), ((), ())), preferred_element_type=jnp.float32
            )
            keep = jnp.broadcast_to(scores[nrows : nrows + 1, :] < limit, (nrows, chunk))
            if half == 0 and any(s == stage for s, _ in row_stage):
                col = lax.broadcasted_iota(jnp.int32, (unit, chunk), 1)
                row = lax.broadcasted_iota(jnp.int32, (unit, chunk), 0)
                off = [
                    col != (row + h * unit if s == stage else -1) for s, h in row_stage
                ]
                keep = keep & jnp.concatenate(off, axis=0)
            weight = jnp.where(keep, jnp.exp(scores[:nrows] * (64.0 / width)), 0.0)
            add_count = jnp.broadcast_to(jnp.sum(weight, axis=1, keepdims=True), count.shape)
            add_pull = jnp.dot(
                weight.astype(jnp.bfloat16), part, preferred_element_type=jnp.float32
            )
            if at:
                count[...] += add_count
                pull[...] += add_pull
            elif carried:
                count[...] = count_in[...] + add_count
                pull[...] = pull_in[...] + add_pull
            else:
                count[...] = add_count
                pull[...] = add_pull
            at += chunk
    if not last:
        return
    valid = rows[pl.ds(0, nrows), 0:128].astype(jnp.float32)[:, 0:1] < limit
    for i in range(nblocks):
        at = i * slots
        ok = valid[at : at + slots]
        cnt = count[pl.ds(at, slots), :]
        near = pull[pl.ds(at, slots), :] / (1.0 + cnt[:, 0:1])
        outs[i][pl.ds(0, slots), :] = jnp.where(ok, near, 0.0).astype(jnp.bfloat16)
        dup = jnp.where(ok, jnp.log1p(cnt), 0.0)
        if slots < 128:
            dup = jnp.concatenate([dup, jnp.zeros((128 - slots, 128), jnp.float32)], axis=0)
        dup = dup.T[0:EXTRA]
        high = dup.astype(jnp.bfloat16).astype(jnp.float32)
        line = lax.broadcasted_iota(jnp.int32, (EXTRA, 128), 0)
        two = jnp.where(line == 0, high, jnp.where(line == 1, dup - high, 0.0))
        outs[i][pl.ds(slots, EXTRA), pl.ds(0, 128)] = two.astype(jnp.bfloat16)


def unpack_kernel(slots, which, carried, pos_ref, *refs):
    refs = list(refs)
    dup_ref, near_ref = refs[-2:]
    blocks = refs[: len(which)]
    n = pos_ref.shape[1]
    pos = pos_ref[...]
    dup = jnp.zeros((EXTRA, n), jnp.float32)
    for i, (k, ref) in enumerate(zip(which, blocks)):
        pick = lax.broadcasted_iota(jnp.int32, (slots, n), 0) + k * slots == pos
        pick = pick.astype(jnp.bfloat16)
        near = lax.dot_general(
            pick,
            ref[pl.ds(0, slots), :],
            (((0,), (0,)), ((), ())),
            preferred_element_type=jnp.float32,
        )
        if i:
            near_ref[...] += near
        elif carried:
            near_ref[...] = refs[len(which) + 1][...] + near
        else:
            near_ref[...] = near
        two = ref[pl.ds(slots, EXTRA), pl.ds(0, 128)][:, :slots]
        dup = dup + jnp.dot(two, pick, preferred_element_type=jnp.float32)
    total = dup[0:1] + dup[1:2]
    dup_ref[...] = refs[len(which)][...] + total if carried else total


def after(value, *deps):
    return lax.optimization_barrier((value,) + deps)[0]


def local(embeddings, cluster):
    n, width = embeddings.shape
    ns, ng = lax.axis_size("shard"), lax.axis_size("grp")
    hi_n = ns // ng
    nb = ns
    slots = 2 * n // ns

    def moved(f):
        return [(s * ng + z, f(s, z)) for s in range(ns) for z in range(ng)]

    def to_owner(dh, dz, sign):
        return moved(
            lambda s, z: ((s // ng + sign * dh) % hi_n * ng + s % ng) * ng + (z + sign * dz) % ng
        )

    def beside(bit):
        return moved(lambda s, z: (s ^ bit) * ng + z)

    hops = [(dh, dz) for dz in hop_order(ng) for dh in range(hi_n)]
    vmem = pl.BlockSpec(memory_space=pltpu.VMEM)
    anyspace = pl.BlockSpec(memory_space=pl.ANY)
    ids = cluster.reshape(1, n)
    pos, *outbox = pl.pallas_call(
        functools.partial(pack_kernel, hi_n, ng, slots),
        out_shape=[jax.ShapeDtypeStruct((1, n), jnp.int32)]
        + [jax.ShapeDtypeStruct((slots, width), jnp.bfloat16)] * nb,
        in_specs=[vmem, vmem],
        out_specs=[vmem] * (nb + 1),
        compiler_params=pltpu.CompilerParams(vmem_limit_bytes=40 * MIB),
        name="pack",
    )(embeddings, ids)

    per = hi_n // 2
    unit = per * slots
    nstage = ng
    inbox = [None] * nb
    own, side, other = {}, {}, {}

    def send(stage, half, *deps):
        got = []
        for k in range(stage * hi_n + half * per, stage * hi_n + (half + 1) * per):
            if k:
                src = after(outbox[k], *deps) if deps else outbox[k]
                inbox[k] = lax.ppermute(src, AXES, to_owner(*hops[k], 1))
            else:
                inbox[k] = outbox[k]
            got.append(inbox[k])
        own[stage, half] = got[0] if per == 1 else jnp.concatenate(got, axis=0)

    def across(stage, half, *deps):
        src = own[stage, half]
        side[stage, half] = lax.ppermute(after(src, *deps) if deps else src, AXES, beside(2))

    def swap(*units):
        both = jnp.concatenate([own[u] for u in units] + [side[u] for u in units], axis=0)
        got = lax.ppermute(both, AXES, beside(1))
        other.setdefault(units[0][0], []).append(got)

    def weigh(row_units, stages, carry=(), last=False, deps=()):
        nblocks = len(row_units) * per
        nrows = len(row_units) * unit
        cols = [(g, [own[g, 0], own[g, 1], side[g, 0], side[g, 1]]) for g in stages]
        cols += [(None, [c]) for g in stages for c in other.get(g, [])]
        layout = [(g, [c.shape[0] for c in cs]) for g, cs in cols]
        total = sum(sum(ns) for _, ns in layout)
        cols = [c for _, cs in cols for c in cs]
        ins = [own[u] for u in row_units] + cols + list(carry)
        if deps:
            ins[0] = after(ins[0], *deps)
        sums = [(nrows, width), (nrows, 128)]
        if last:
            out_shape = [jax.ShapeDtypeStruct((slots + EXTRA, width), jnp.bfloat16)] * nblocks
        else:
            out_shape = [jax.ShapeDtypeStruct(t, jnp.float32) for t in sums]
        return pl.pallas_call(
            functools.partial(
                weigh_kernel, layout, row_units, slots, nblocks, bool(carry), last
            ),
            out_shape=out_shape,
            in_specs=[anyspace] * (len(ins) - len(carry)) + [vmem] * len(carry),
            out_specs=[vmem] * len(out_shape),
            input_output_aliases=(
                {len(ins) - 2: 0, len(ins) - 1: 1} if carry and not last else {}
            ),
            scratch_shapes=[
                pltpu.VMEM((total, width), jnp.bfloat16),
                pltpu.VMEM((nrows + 16, width), jnp.bfloat16),
            ]
            + ([pltpu.VMEM(t, jnp.float32) for t in sums] if last else [])
            + [pltpu.SemaphoreType.DMA((len(ins),))],
            compiler_params=pltpu.CompilerParams(vmem_limit_bytes=48 * MIB),
            cost_estimate=pl.CostEstimate(
                flops=4 * nrows * total * width if last else 0,
                bytes_accessed=2 * total * width if last else 0,
                transcendentals=nrows * total if last else 0,
            ),
            name="weigh",
        )(*ins)

    send(1, 0)
    send(1, 1)
    send(0, 0)
    across(0, 0)
    send(0, 1)
    across(0, 1, side[0, 0])
    send(2, 0, own[0, 1])
    across(1, 0, own[1, 0])
    send(2, 1, own[1, 0])
    across(1, 1, side[0, 1])
    send(3, 0, own[1, 1])
    swap((0, 0), (0, 1))
    across(2, 0, side[1, 0])
    send(3, 1, own[2, 0])
    across(2, 1, side[1, 1])
    swap((1, 0), (1, 1))
    across(3, 0, side[2, 0])
    across(3, 1, side[2, 1])
    swap((2, 0), (2, 1))
    swap((3, 0))
    swap((3, 1))
    parts = [[(1, 0), (1, 1)], [(2, 0), (2, 1)], [(3, 0), (3, 1), (0, 1), (0, 0)]]
    result = [None] * nb
    order, deps = [], ()
    for part in parts:
        outs = weigh(part, list(range(nstage)), (), True, deps)
        deps = outs[:1]
        blocks = [g * hi_n + h * per + i for g, h in part for i in range(per)]
        for k, r in zip(blocks, outs):
            result[k] = r
        order += blocks
    back = [result[0]] + [None] * (nb - 1)
    for b in order:
        if b:
            back[b] = lax.ppermute(result[b], AXES, to_owner(*hops[b], -1))

    def unpack(which, carry=()):
        return pl.pallas_call(
            functools.partial(unpack_kernel, slots, which, bool(carry)),
            out_shape=[
                jax.ShapeDtypeStruct((1, n), jnp.float32),
                jax.ShapeDtypeStruct((n, width), jnp.float32),
            ],
            in_specs=[vmem] * (1 + len(which) + len(carry)),
            out_specs=[vmem, vmem],
            compiler_params=pltpu.CompilerParams(vmem_limit_bytes=40 * MIB),
            name="unpack",
        )(pos, *[back[k] for k in which], *carry)

    late = [b for g, h in parts[2][:3] for b in range(g * hi_n + h * per, g * hi_n + (h + 1) * per)]
    dup, near = unpack(late, unpack([b for b in range(nb) if b not in late]))
    return dup.reshape(n), near


def solution(mesh):
    return jax.shard_map(
        local,
        mesh=mesh,
        in_specs=(P(("shard", "grp"), None), P(("shard", "grp"), None)),
        out_specs=(P(("shard", "grp")), P(("shard", "grp"), None)),
        check_vma=False,
    )
```

```python
import functools

import jax
import jax.numpy as jnp
from jax import lax
from jax.experimental import pallas as pl
from jax.experimental.pallas import tpu as pltpu
from jax.sharding import PartitionSpec as P

AXES = ("shard", "grp")
MIB = 1 << 20


def hop_order(ng):
    return sorted(range(ng), key=lambda d: (min(d, ng - d), d))


def write_blocks(first, slots, pos, used, units, out_refs):
    n, width = units.shape
    mark = float(2.0 * width**0.5)
    for i, ref in enumerate(out_refs):
        k = first + i
        pick = lax.broadcasted_iota(jnp.int32, (slots, n), 0) + k * slots == pos
        rows = jnp.dot(pick.astype(jnp.bfloat16), units, preferred_element_type=jnp.float32)
        empty = lax.broadcasted_iota(jnp.int32, (slots, width), 0) >= used[k : k + 1, 0:1]
        column = lax.broadcasted_iota(jnp.int32, (slots, width), 1)
        ref[...] = jnp.where(empty & (column == 0), mark, rows).astype(jnp.bfloat16)


def pack_kernel(hi_n, ng, slots, first, emb_ref, ids_ref, pos_ref, used_ref, units_ref, *out_refs):
    n, width = emb_ref.shape
    nb = hi_n * ng
    hi = lax.axis_index("shard") // ng
    z = lax.axis_index("grp")
    ids = ids_ref[...]
    blk = jnp.zeros((1, n), jnp.int32)
    for k, dz in enumerate(hop_order(ng)):
        for dh in range(hi_n):
            owner = lax.rem(hi + dh, hi_n) * ng + lax.rem(z + dz, ng)
            blk = jnp.where(ids == owner, k * hi_n + dh, blk)
    onehot = lax.broadcasted_iota(jnp.int32, (nb, n), 0) == blk
    upto = lax.broadcasted_iota(jnp.int32, (n, n), 0) <= lax.broadcasted_iota(jnp.int32, (n, n), 1)
    cum = jnp.dot(
        onehot.astype(jnp.bfloat16), upto.astype(jnp.bfloat16), preferred_element_type=jnp.float32
    )
    rank = jnp.sum(jnp.where(onehot, cum, 0.0), axis=0, keepdims=True).astype(jnp.int32) - 1
    pos = blk * slots + rank
    used = cum[:, n - 1 : n].astype(jnp.int32)
    pos_ref[...] = pos
    used_ref[...] = jnp.broadcast_to(used, used_ref.shape)
    emb = emb_ref[...]
    scale = lax.rsqrt(jnp.mean(emb * emb, axis=1, keepdims=True) + 1e-06)
    units = (emb * scale).astype(jnp.bfloat16)
    units_ref[...] = units
    write_blocks(first, slots, pos, used, units, out_refs)


def pack_rest_kernel(slots, skip, pos_ref, used_ref, units_ref, *out_refs):
    units, pos, used = units_ref[...], pos_ref[...], used_ref[...]
    start, stop = skip
    write_blocks(0, slots, pos, used, units, out_refs[:start])
    write_blocks(stop, slots, pos, used, units, out_refs[start:])


def weigh_kernel(layout, row_stage, unit, slots, ng, hops, summed, carried, last, *refs):
    refs = list(refs)

    def take(count):
        got = refs[:count]
        del refs[:count]
        return got

    row_in = take(sum(c for _, _, c in row_stage))
    cols = take(sum(c for _, c in layout))
    pull_in, count_in = take(2) if summed else (None, None)
    dups_in = take(1) if carried else None
    if last:
        outs = take(len(hops))
        dups, pull, count = refs
    else:
        pull, count = refs
    width = row_in[0].shape[1]
    nrows = len(row_stage) * unit
    limit = 1.5 * width**0.5
    probe = lax.broadcasted_iota(jnp.int32, (16, width), 1) == 0
    rows = jnp.concatenate([r[...] for r in row_in] + [probe.astype(jnp.bfloat16)], axis=0)
    for at, (stage, narr) in enumerate(layout):
        part = jnp.concatenate([c[...] for c in cols[:narr]], axis=0)
        del cols[:narr]
        chunk = part.shape[0]
        scores = lax.dot_general(
            rows, part, (((1,), (1,)), ((), ())), preferred_element_type=jnp.float32
        )
        keep = jnp.broadcast_to(scores[nrows : nrows + 1, :] < limit, (nrows, chunk))
        if any(s == stage for s, _, _ in row_stage):
            col = lax.broadcasted_iota(jnp.int32, (unit, chunk), 1)
            row = lax.broadcasted_iota(jnp.int32, (unit, chunk), 0)
            off = [col != (row + h * unit if s == stage else -1) for s, h, _ in row_stage]
            keep = keep & jnp.concatenate(off, axis=0)
        weight = jnp.where(keep, jnp.exp(scores[:nrows] * (64.0 / width)), 0.0)
        add_count = jnp.broadcast_to(jnp.sum(weight, axis=1, keepdims=True), count.shape)
        add_pull = jnp.dot(weight.astype(jnp.bfloat16), part, preferred_element_type=jnp.float32)
        if at:
            count[...] += add_count
            pull[...] += add_pull
        elif summed:
            count[...] = count_in[...] + add_count
            pull[...] = pull_in[...] + add_pull
        else:
            count[...] = add_count
            pull[...] = add_pull
    if not last:
        return
    dups[...] = dups_in[0][...] if carried else jnp.zeros(dups.shape, jnp.float32)
    hi_n = dups.shape[0] // ng
    hi, z = lax.axis_index("shard") // ng, lax.axis_index("grp")
    valid = rows[:nrows, 0:128].astype(jnp.float32)[:, 0:1] < limit
    for i in range(len(hops)):
        at = i * slots
        ok = valid[at : at + slots]
        cnt = count[pl.ds(at, slots), :]
        near = pull[pl.ds(at, slots), :] / (1.0 + cnt[:, 0:1])
        outs[i][...] = jnp.where(ok, near, 0.0).astype(jnp.bfloat16)
        dup = jnp.where(ok, jnp.log1p(cnt), 0.0)
        if slots < 128:
            dup = jnp.concatenate([dup, jnp.zeros((128 - slots, 128), jnp.float32)], axis=0)
        dh, dz = hops[i]
        home = lax.rem(hi + hi_n - dh, hi_n) * ng + lax.rem(z + ng - dz, ng)
        dups[pl.ds(home, 1), :] = dup.T[0:1]


def unpack_kernel(slots, which, last, hi_n, ng, pos_ref, *refs):
    refs = list(refs)
    nwhich = len(which)
    pos = pos_ref[...]
    n = pos.shape[1]

    def pick(k):
        at = lax.broadcasted_iota(jnp.int32, (slots, n), 0) + k * slots
        return (at == pos).astype(jnp.bfloat16)

    picks = jnp.concatenate([pick(k) for k in which], axis=0)
    rows = jnp.concatenate([r[...] for r in refs[:nwhich]], axis=0)
    if not last:
        dups, dup_ref, near_ref = refs[nwhich:]
        hi, z = lax.axis_index("shard") // ng, lax.axis_index("grp")
        line = lax.broadcasted_iota(jnp.int32, (8, 128), 0)
        dup = jnp.zeros((8, n), jnp.float32)
        for k, (dh, dz) in enumerate((dh, dz) for dz in hop_order(ng) for dh in range(hi_n)):
            owner = lax.rem(hi + dh, hi_n) * ng + lax.rem(z + dz, ng)
            row = jnp.broadcast_to(dups[pl.ds(owner, 1), :], (8, 128))
            high = row.astype(jnp.bfloat16).astype(jnp.float32)
            two = jnp.where(line == 0, high, jnp.where(line == 1, row - high, 0.0))
            two = two.astype(jnp.bfloat16)[:, :slots]
            dup = dup + jnp.dot(two, pick(k), preferred_element_type=jnp.float32)
        dup_ref[...] = dup[0:1] + dup[1:2]
        near_ref[...] = lax.dot_general(
            picks, rows, (((0,), (0,)), ((), ())), preferred_element_type=jnp.float32
        )
        return
    near_in, near_ref, near, sems = refs[nwhich:]
    step = n // 4
    copies = []
    for i in range(4):
        at = pl.ds(i * step, step)
        near[at, :] = near_in[at, :] + lax.dot_general(
            picks[:, i * step : (i + 1) * step],
            rows,
            (((0,), (0,)), ((), ())),
            preferred_element_type=jnp.float32,
        )
        copies.append(pltpu.make_async_copy(near.at[at], near_ref.at[at], sems.at[i]))
        copies[-1].start()
    for c in copies:
        c.wait()


def after(value, *deps):
    return lax.optimization_barrier((value,) + deps)[0]


def local(embeddings, cluster):
    n, width = embeddings.shape
    ns, ng = lax.axis_size("shard"), lax.axis_size("grp")
    hi_n = ns // ng
    nb = ns
    slots = 2 * n // ns

    def moved(f):
        return [(s * ng + z, f(s, z)) for s in range(ns) for z in range(ng)]

    def to_owner(dh, dz, sign):
        return moved(
            lambda s, z: ((s // ng + sign * dh) % hi_n * ng + s % ng) * ng + (z + sign * dz) % ng
        )

    def beside(bit):
        return moved(lambda s, z: (s ^ bit) * ng + z)

    hops = [(dh, dz) for dz in hop_order(ng) for dh in range(hi_n)]
    vmem = pl.BlockSpec(memory_space=pltpu.VMEM)
    hbm = pl.BlockSpec(memory_space=pltpu.HBM)
    ids = cluster.reshape(1, n)
    block = jax.ShapeDtypeStruct((slots, width), jnp.bfloat16)
    small = pltpu.CompilerParams(vmem_limit_bytes=16 * MIB)
    pos, used, units, *outbox = pl.pallas_call(
        functools.partial(pack_kernel, hi_n, ng, slots, hi_n),
        out_shape=[
            jax.ShapeDtypeStruct((1, n), jnp.int32),
            jax.ShapeDtypeStruct((nb, 128), jnp.int32),
            jax.ShapeDtypeStruct((n, width), jnp.bfloat16),
        ]
        + [block] * hi_n,
        in_specs=[vmem, vmem],
        out_specs=[vmem] * (hi_n + 3),
        compiler_params=small,
        name="pack",
    )(embeddings, ids)
    rest = pl.pallas_call(
        functools.partial(pack_rest_kernel, slots, (hi_n, 2 * hi_n)),
        out_shape=[block] * (nb - hi_n),
        in_specs=[vmem] * 3,
        out_specs=[vmem] * (nb - hi_n),
        compiler_params=small,
        name="pack_rest",
    )(pos, used, units)
    outbox = [*rest[:hi_n], *outbox, *rest[hi_n:]]

    per = hi_n // 2
    unit = per * slots
    nstage = ng
    own, side, other = {}, {}, {}

    def send(stage, half, *deps, cut=1):
        ks = blocks_of((stage, half))
        whole = [outbox[k] for k in ks]
        if cut > 1 and per == 1:
            pieces = [(ks[0], whole[0][i * unit // cut : (i + 1) * unit // cut]) for i in range(cut)]
        else:
            pieces = list(zip(ks, whole))
        got = []
        for k, src in pieces:
            if k:
                src = lax.ppermute(after(src, *deps) if deps else src, AXES, to_owner(*hops[k], 1))
            got.append(src)
        each = len(got) // cut
        own[stage, half] = [
            got[i] if each == 1 else jnp.concatenate(got[i : i + each], axis=0)
            for i in range(0, len(got), each)
        ]

    def across(stage, half, *deps):
        side[stage, half] = [
            lax.ppermute(after(src, *deps) if deps else src, AXES, beside(2))
            for src in own[stage, half]
        ]

    def swap(*units, deps=()):
        both = jnp.concatenate([a for t in (own, side) for u in units for a in t[u]], axis=0)
        got = lax.ppermute(after(both, *deps) if deps else both, AXES, beside(1))
        other.setdefault(units[0][0], []).append(got)

    def blocks_of(unit):
        start = unit[0] * hi_n + unit[1] * per
        return range(start, start + per)

    def weigh(row_units, stages, sums=(), dups=(), last=True, deps=()):
        nrows = len(row_units) * unit
        layout, cols = [], []
        for g in stages:
            cs = own[g, 0] + own[g, 1] + side[g, 0] + side[g, 1]
            layout.append((g, len(cs)))
            cols += cs
        for g in stages:
            layout.append((None, len(other[g])))
            cols += other[g]
        total = sum(c.shape[0] for c in cols)
        row_in = [a for u in row_units for a in own[u]]
        if deps:
            row_in[0] = after(row_in[0], *deps)
        row_stage = [(g, h, len(own[g, h])) for g, h in row_units]
        ks = [k for u in row_units for k in blocks_of(u)]
        acc = [(nrows, width), (nrows, 128)]
        ins = row_in + cols + list(sums) + list(dups)
        if last:
            out_shape = [block] * len(ks) + [jax.ShapeDtypeStruct((nb, 128), jnp.float32)]
        else:
            out_shape = [jax.ShapeDtypeStruct(t, jnp.float32) for t in acc]
        return pl.pallas_call(
            functools.partial(
                weigh_kernel,
                layout,
                row_stage,
                unit,
                slots,
                ng,
                [hops[k] for k in ks],
                bool(sums),
                bool(dups),
                last,
            ),
            out_shape=out_shape,
            in_specs=[vmem] * len(ins),
            out_specs=[vmem] * len(out_shape),
            scratch_shapes=[pltpu.VMEM(t, jnp.float32) for t in acc] if last else [],
            compiler_params=pltpu.CompilerParams(vmem_limit_bytes=32 * MIB),
            cost_estimate=pl.CostEstimate(
                flops=4 * nrows * total * width,
                bytes_accessed=2 * total * width,
                transcendentals=nrows * total,
            ),
            name="weigh",
        )(*ins)

    send(0, 0)
    send(1, 0)
    send(1, 1)
    send(2, 0)
    send(0, 1)
    across(0, 0, *own[1, 0])
    across(0, 1)
    across(1, 0)
    across(1, 1, *side[0, 0])
    send(2, 1, *own[1, 0])
    send(3, 0, *own[1, 1])
    send(3, 1, *own[2, 0])
    across(2, 0, *side[1, 0], *side[0, 1])
    across(2, 1, *side[1, 1])
    across(3, 0, *side[2, 0])
    across(3, 1, *side[2, 1])
    swap((0, 0), (0, 1))
    swap((1, 0), (1, 1))
    swap((2, 0), (2, 1))
    swap((3, 0))
    parts = [[(1, 0), (1, 1)], [(2, 0), (2, 1)], [(3, 0), (3, 1), (0, 1), (0, 0)]]
    stages = list(range(nstage))
    swap((3, 1))
    early, sums = [], ()
    result = [None] * nb
    order, dups, deps = [], (), ()
    for part in parts:
        todo = [g for g in stages if g not in early]
        *outs, dup = weigh(part, todo, sums, dups, deps=deps)
        early, sums, dups, deps = [], (), (dup,), outs[:1]
        blocks = [k for u in part for k in blocks_of(u)]
        for k, r in zip(blocks, outs):
            result[k] = r
        order += blocks
    back = [result[0]] + [None] * (nb - 1)
    for b in order:
        if b:
            back[b] = lax.ppermute(result[b], AXES, to_owner(*hops[b], -1))

    same = [
        [((h * ng + lo) * ng) + z for h in range(hi_n) for z in range(ng)] for lo in range(ng)
    ]
    dups = lax.all_to_all(*dups, AXES, 0, 0, tiled=True, axis_index_groups=same)

    def unpack(which, also, last):
        near = jax.ShapeDtypeStruct((n, width), jnp.float32)
        scratch = [pltpu.VMEM((n, width), jnp.float32), pltpu.SemaphoreType.DMA((4,))]
        return pl.pallas_call(
            functools.partial(unpack_kernel, slots, which, last, hi_n, ng),
            out_shape=[near] if last else [jax.ShapeDtypeStruct((1, n), jnp.float32), near],
            in_specs=[vmem] * (2 + len(which)),
            out_specs=[hbm] if last else [vmem, vmem],
            scratch_shapes=scratch if last else [],
            compiler_params=pltpu.CompilerParams(vmem_limit_bytes=16 * MIB),
            name="unpack",
        )(pos, *[back[k] for k in which], also)

    late = [k for u in parts[2][:3] for k in blocks_of(u)]
    dup, near = unpack([b for b in range(nb) if b not in late], dups, False)
    (near,) = unpack(late, near, True)
    return dup.reshape(n), near


def solution(mesh):
    return jax.shard_map(
        local,
        mesh=mesh,
        in_specs=(P(("shard", "grp"), None), P(("shard", "grp"), None)),
        out_specs=(P(("shard", "grp")), P(("shard", "grp"), None)),
        check_vma=False,
    )
```

```python
import functools

import jax
import jax.numpy as jnp
from jax import lax
from jax.experimental import pallas as pl
from jax.experimental.pallas import tpu as pltpu
from jax.sharding import PartitionSpec as P

AXES = ("shard", "grp")
MIB = 1 << 20


def hop_order(ng):
    return sorted(range(ng), key=lambda d: (min(d, ng - d), d))


def write_blocks(first, slots, pos, used, units, out_refs):
    n, width = units.shape
    mark = float(2.0 * width**0.5)
    for i, ref in enumerate(out_refs):
        k = first + i
        pick = lax.broadcasted_iota(jnp.int32, (slots, n), 0) + k * slots == pos
        rows = jnp.dot(pick.astype(jnp.bfloat16), units, preferred_element_type=jnp.float32)
        empty = lax.broadcasted_iota(jnp.int32, (slots, width), 0) >= used[k : k + 1, 0:1]
        column = lax.broadcasted_iota(jnp.int32, (slots, width), 1)
        ref[...] = jnp.where(empty & (column == 0), mark, rows).astype(jnp.bfloat16)


def pack_kernel(hi_n, ng, slots, first, emb_ref, ids_ref, pos_ref, used_ref, units_ref, *out_refs):
    n, width = emb_ref.shape
    nb = hi_n * ng
    hi = lax.axis_index("shard") // ng
    z = lax.axis_index("grp")
    ids = ids_ref[...]
    blk = jnp.zeros((1, n), jnp.int32)
    for k, dz in enumerate(hop_order(ng)):
        for dh in range(hi_n):
            owner = lax.rem(hi + dh, hi_n) * ng + lax.rem(z + dz, ng)
            blk = jnp.where(ids == owner, k * hi_n + dh, blk)
    onehot = lax.broadcasted_iota(jnp.int32, (nb, n), 0) == blk
    upto = lax.broadcasted_iota(jnp.int32, (n, n), 0) <= lax.broadcasted_iota(jnp.int32, (n, n), 1)
    cum = jnp.dot(
        onehot.astype(jnp.bfloat16), upto.astype(jnp.bfloat16), preferred_element_type=jnp.float32
    )
    rank = jnp.sum(jnp.where(onehot, cum, 0.0), axis=0, keepdims=True).astype(jnp.int32) - 1
    pos = blk * slots + rank
    used = cum[:, n - 1 : n].astype(jnp.int32)
    pos_ref[...] = pos
    used_ref[...] = jnp.broadcast_to(used, used_ref.shape)
    emb = emb_ref[...]
    scale = lax.rsqrt(jnp.mean(emb * emb, axis=1, keepdims=True) + 1e-06)
    units = (emb * scale).astype(jnp.bfloat16)
    units_ref[...] = units
    write_blocks(first, slots, pos, used, units, out_refs)


def pack_rest_kernel(slots, skip, pos_ref, used_ref, units_ref, *out_refs):
    units, pos, used = units_ref[...], pos_ref[...], used_ref[...]
    start, stop = skip
    write_blocks(0, slots, pos, used, units, out_refs[:start])
    write_blocks(stop, slots, pos, used, units, out_refs[start:])


def weigh_kernel(layout, row_stage, unit, slots, ng, hops, summed, carried, last, *refs):
    refs = list(refs)

    def take(count):
        got = refs[:count]
        del refs[:count]
        return got

    row_in = take(sum(c for _, _, c in row_stage))
    cols = take(sum(c for _, c in layout))
    pull_in, count_in = take(2) if summed else (None, None)
    dups_in = take(1) if carried else None
    if last:
        outs = take(len(hops))
        dups, pull, count = refs
    else:
        pull, count = refs
    width = row_in[0].shape[1]
    nrows = len(row_stage) * unit
    limit = 1.5 * width**0.5
    probe = lax.broadcasted_iota(jnp.int32, (16, width), 1) == 0
    rows = jnp.concatenate([r[...] for r in row_in] + [probe.astype(jnp.bfloat16)], axis=0)
    for at, (stage, narr) in enumerate(layout):
        part = jnp.concatenate([c[...] for c in cols[:narr]], axis=0)
        del cols[:narr]
        chunk = part.shape[0]
        scores = lax.dot_general(
            rows, part, (((1,), (1,)), ((), ())), preferred_element_type=jnp.float32
        )
        keep = jnp.broadcast_to(scores[nrows : nrows + 1, :] < limit, (nrows, chunk))
        if any(s == stage for s, _, _ in row_stage):
            col = lax.broadcasted_iota(jnp.int32, (unit, chunk), 1)
            row = lax.broadcasted_iota(jnp.int32, (unit, chunk), 0)
            off = [col != (row + h * unit if s == stage else -1) for s, h, _ in row_stage]
            keep = keep & jnp.concatenate(off, axis=0)
        weight = jnp.where(keep, jnp.exp(scores[:nrows] * (64.0 / width)), 0.0)
        add_count = jnp.broadcast_to(jnp.sum(weight, axis=1, keepdims=True), count.shape)
        add_pull = jnp.dot(weight.astype(jnp.bfloat16), part, preferred_element_type=jnp.float32)
        if at:
            count[...] += add_count
            pull[...] += add_pull
        elif summed:
            count[...] = count_in[...] + add_count
            pull[...] = pull_in[...] + add_pull
        else:
            count[...] = add_count
            pull[...] = add_pull
    if not last:
        return
    dups[...] = dups_in[0][...] if carried else jnp.zeros(dups.shape, jnp.float32)
    hi_n = dups.shape[0] // ng
    hi, z = lax.axis_index("shard") // ng, lax.axis_index("grp")
    valid = rows[:nrows, 0:128].astype(jnp.float32)[:, 0:1] < limit
    for i in range(len(hops)):
        at = i * slots
        ok = valid[at : at + slots]
        cnt = count[pl.ds(at, slots), :]
        near = pull[pl.ds(at, slots), :] / (1.0 + cnt[:, 0:1])
        outs[i][...] = jnp.where(ok, near, 0.0).astype(jnp.bfloat16)
        dup = jnp.where(ok, jnp.log1p(cnt), 0.0)
        if slots < 128:
            dup = jnp.concatenate([dup, jnp.zeros((128 - slots, 128), jnp.float32)], axis=0)
        dh, dz = hops[i]
        home = lax.rem(hi + hi_n - dh, hi_n) * ng + lax.rem(z + ng - dz, ng)
        dups[pl.ds(home, 1), :] = dup.T[0:1]


def unpack_kernel(slots, which, last, hi_n, ng, pos_ref, *refs):
    refs = list(refs)
    nwhich = len(which)
    pos = pos_ref[...]
    n = pos.shape[1]

    def pick(k):
        at = lax.broadcasted_iota(jnp.int32, (slots, n), 0) + k * slots
        return (at == pos).astype(jnp.bfloat16)

    picks = jnp.concatenate([pick(k) for k in which], axis=0)
    rows = jnp.concatenate([r[...] for r in refs[:nwhich]], axis=0)
    if not last:
        (near_ref,) = refs[nwhich:]
        near_ref[...] = lax.dot_general(
            picks, rows, (((0,), (0,)), ((), ())), preferred_element_type=jnp.float32
        )
        return
    near_in, dups, near_ref, dup_ref, near, sems = refs[nwhich:]
    step = n // 4
    copies = []
    for i in range(4):
        at = pl.ds(i * step, step)
        near[at, :] = near_in[at, :] + lax.dot_general(
            picks[:, i * step : (i + 1) * step],
            rows,
            (((0,), (0,)), ((), ())),
            preferred_element_type=jnp.float32,
        )
        copies.append(pltpu.make_async_copy(near.at[at], near_ref.at[at], sems.at[i]))
        copies[-1].start()
    hi, z = lax.axis_index("shard") // ng, lax.axis_index("grp")
    line = lax.broadcasted_iota(jnp.int32, (8, 128), 0)
    dup = jnp.zeros((8, n), jnp.float32)
    for k, (dh, dz) in enumerate((dh, dz) for dz in hop_order(ng) for dh in range(hi_n)):
        owner = lax.rem(hi + dh, hi_n) * ng + lax.rem(z + dz, ng)
        row = jnp.broadcast_to(dups[pl.ds(owner, 1), :], (8, 128))
        high = row.astype(jnp.bfloat16).astype(jnp.float32)
        two = jnp.where(line == 0, high, jnp.where(line == 1, row - high, 0.0))
        two = two.astype(jnp.bfloat16)[:, :slots]
        dup = dup + jnp.dot(two, pick(k), preferred_element_type=jnp.float32)
    dup_ref[...] = dup[0:1] + dup[1:2]
    for c in copies:
        c.wait()


def after(value, *deps):
    return lax.optimization_barrier((value,) + deps)[0]


def local(embeddings, cluster):
    n, width = embeddings.shape
    ns, ng = lax.axis_size("shard"), lax.axis_size("grp")
    hi_n = ns // ng
    nb = ns
    slots = 2 * n // ns

    def moved(f):
        return [(s * ng + z, f(s, z)) for s in range(ns) for z in range(ng)]

    def to_owner(dh, dz, sign):
        return moved(
            lambda s, z: ((s // ng + sign * dh) % hi_n * ng + s % ng) * ng + (z + sign * dz) % ng
        )

    def beside(bit):
        return moved(lambda s, z: (s ^ bit) * ng + z)

    hops = [(dh, dz) for dz in hop_order(ng) for dh in range(hi_n)]
    vmem = pl.BlockSpec(memory_space=pltpu.VMEM)
    hbm = pl.BlockSpec(memory_space=pltpu.HBM)
    ids = cluster.reshape(1, n)
    block = jax.ShapeDtypeStruct((slots, width), jnp.bfloat16)
    small = pltpu.CompilerParams(vmem_limit_bytes=16 * MIB)
    pos, used, units, *outbox = pl.pallas_call(
        functools.partial(pack_kernel, hi_n, ng, slots, hi_n),
        out_shape=[
            jax.ShapeDtypeStruct((1, n), jnp.int32),
            jax.ShapeDtypeStruct((nb, 128), jnp.int32),
            jax.ShapeDtypeStruct((n, width), jnp.bfloat16),
        ]
        + [block] * hi_n,
        in_specs=[vmem, vmem],
        out_specs=[vmem] * (hi_n + 3),
        compiler_params=small,
        name="pack",
    )(embeddings, ids)
    rest = pl.pallas_call(
        functools.partial(pack_rest_kernel, slots, (hi_n, 2 * hi_n)),
        out_shape=[block] * (nb - hi_n),
        in_specs=[vmem] * 3,
        out_specs=[vmem] * (nb - hi_n),
        compiler_params=small,
        name="pack_rest",
    )(pos, used, units)
    outbox = [*rest[:hi_n], *outbox, *rest[hi_n:]]

    per = hi_n // 2
    unit = per * slots
    nstage = ng
    own, side, other = {}, {}, {}

    def send(stage, half, *deps, cut=1):
        ks = blocks_of((stage, half))
        whole = [outbox[k] for k in ks]
        if cut > 1 and per == 1:
            pieces = [(ks[0], whole[0][i * unit // cut : (i + 1) * unit // cut]) for i in range(cut)]
        else:
            pieces = list(zip(ks, whole))
        got = []
        for k, src in pieces:
            if k:
                src = lax.ppermute(after(src, *deps) if deps else src, AXES, to_owner(*hops[k], 1))
            got.append(src)
        each = len(got) // cut
        own[stage, half] = [
            got[i] if each == 1 else jnp.concatenate(got[i : i + each], axis=0)
            for i in range(0, len(got), each)
        ]

    def across(stage, half, *deps):
        side[stage, half] = [
            lax.ppermute(after(src, *deps) if deps else src, AXES, beside(2))
            for src in own[stage, half]
        ]

    def swap(*units, deps=()):
        both = jnp.concatenate([a for t in (own, side) for u in units for a in t[u]], axis=0)
        got = lax.ppermute(after(both, *deps) if deps else both, AXES, beside(1))
        other.setdefault(units[0][0], []).append(got)

    def pieces(g):
        other[g] = [
            lax.ppermute(a, AXES, beside(1)) for t in (own, side) for h in range(2) for a in t[g, h]
        ]

    def blocks_of(unit):
        start = unit[0] * hi_n + unit[1] * per
        return range(start, start + per)

    def weigh(row_units, stages, sums=(), dups=(), last=True, deps=()):
        nrows = len(row_units) * unit
        layout, cols = [], []
        for g in stages:
            cs = own[g, 0] + own[g, 1] + side[g, 0] + side[g, 1]
            layout.append((g, len(cs)))
            cols += cs
        for g in stages:
            layout.append((None, len(other[g])))
            cols += other[g]
        total = sum(c.shape[0] for c in cols)
        row_in = [a for u in row_units for a in own[u]]
        if deps:
            row_in[0] = after(row_in[0], *deps)
        row_stage = [(g, h, len(own[g, h])) for g, h in row_units]
        ks = [k for u in row_units for k in blocks_of(u)]
        acc = [(nrows, width), (nrows, 128)]
        ins = row_in + cols + list(sums) + list(dups)
        if last:
            out_shape = [block] * len(ks) + [jax.ShapeDtypeStruct((nb, 128), jnp.float32)]
        else:
            out_shape = [jax.ShapeDtypeStruct(t, jnp.float32) for t in acc]
        return pl.pallas_call(
            functools.partial(
                weigh_kernel,
                layout,
                row_stage,
                unit,
                slots,
                ng,
                [hops[k] for k in ks],
                bool(sums),
                bool(dups),
                last,
            ),
            out_shape=out_shape,
            in_specs=[vmem] * len(ins),
            out_specs=[vmem] * len(out_shape),
            scratch_shapes=[pltpu.VMEM(t, jnp.float32) for t in acc] if last else [],
            compiler_params=pltpu.CompilerParams(vmem_limit_bytes=32 * MIB),
            cost_estimate=pl.CostEstimate(
                flops=4 * nrows * total * width if last else 0,
                bytes_accessed=2 * total * width if last else 0,
                transcendentals=nrows * total if last else 0,
            ),
            name="weigh",
        )(*ins)

    send(0, 0)
    send(1, 0)
    send(1, 1)
    send(2, 0)
    send(0, 1)
    across(0, 0, *own[1, 0])
    across(0, 1)
    across(1, 0)
    across(1, 1, *side[0, 0])
    send(2, 1, *own[1, 0])
    send(3, 0, *own[1, 1])
    send(3, 1, *own[2, 0])
    across(2, 0, *side[1, 0], *side[0, 1])
    across(2, 1, *side[1, 1])
    across(3, 0, *side[2, 0])
    across(3, 1, *side[2, 1])
    pieces(0)
    pieces(1)
    swap((2, 0), (2, 1))
    swap((3, 0))
    parts = [[(1, 0), (1, 1)], [(2, 0), (2, 1)], [(3, 0), (3, 1), (0, 1), (0, 0)]]
    stages = list(range(nstage))
    early = [0, 1]
    sums = weigh(parts[0], early, last=False, deps=side[3, 0])
    swap((3, 1), deps=sums[1:])
    result = [None] * nb
    order, dups, deps = [], (), ()
    for part in parts:
        todo = [g for g in stages if g not in early]
        *outs, dup = weigh(part, todo, sums, dups, deps=deps)
        early, sums, dups, deps = [], (), (dup,), outs[:1]
        blocks = [k for u in part for k in blocks_of(u)]
        for k, r in zip(blocks, outs):
            result[k] = r
        order += blocks
    back = [result[0]] + [None] * (nb - 1)
    for b in order:
        if b:
            back[b] = lax.ppermute(result[b], AXES, to_owner(*hops[b], -1))

    same = [
        [((h * ng + lo) * ng) + z for h in range(hi_n) for z in range(ng)] for lo in range(ng)
    ]

    def unpack(which, also, last):
        near = jax.ShapeDtypeStruct((n, width), jnp.float32)
        scratch = [pltpu.VMEM((n, width), jnp.float32), pltpu.SemaphoreType.DMA((4,))]
        return pl.pallas_call(
            functools.partial(unpack_kernel, slots, which, last, hi_n, ng),
            out_shape=[near, jax.ShapeDtypeStruct((1, n), jnp.float32)] if last else [near],
            in_specs=[vmem] * (1 + len(which) + len(also)),
            out_specs=[hbm, vmem] if last else [vmem],
            scratch_shapes=scratch if last else [],
            compiler_params=small,
            name="unpack",
        )(pos, *[back[k] for k in which], *also)

    late = [k for u in parts[2][:3] for k in blocks_of(u)]
    (near,) = unpack([b for b in range(nb) if b not in late], (), False)
    dups = lax.all_to_all(after(*dups, near), AXES, 0, 0, tiled=True, axis_index_groups=same)
    near, dup = unpack(late, (near, dups), True)
    return dup.reshape(n), near


def solution(mesh):
    return jax.shard_map(
        local,
        mesh=mesh,
        in_specs=(P(("shard", "grp"), None), P(("shard", "grp"), None)),
        out_specs=(P(("shard", "grp")), P(("shard", "grp"), None)),
        check_vma=False,
    )
```

```python
import functools

import jax
import jax.numpy as jnp
from jax import lax
from jax.experimental import pallas as pl
from jax.experimental.pallas import tpu as pltpu
from jax.sharding import PartitionSpec as P

AXES = ("shard", "grp")
MIB = 1 << 20


def hop_order(ng):
    return sorted(range(ng), key=lambda d: (min(d, ng - d), d))


def write_blocks(first, slots, pos, used, units, out_refs):
    n, width = units.shape
    mark = float(2.0 * width**0.5)
    for i, ref in enumerate(out_refs):
        k = first + i
        pick = lax.broadcasted_iota(jnp.int32, (slots, n), 0) + k * slots == pos
        rows = jnp.dot(pick.astype(jnp.bfloat16), units, preferred_element_type=jnp.float32)
        empty = lax.broadcasted_iota(jnp.int32, (slots, width), 0) >= used[k : k + 1, 0:1]
        column = lax.broadcasted_iota(jnp.int32, (slots, width), 1)
        ref[...] = jnp.where(empty & (column == 0), mark, rows).astype(jnp.bfloat16)


def pack_kernel(hi_n, ng, slots, first, emb_ref, ids_ref, pos_ref, used_ref, units_ref, *out_refs):
    n, width = emb_ref.shape
    nb = hi_n * ng
    hi = lax.axis_index("shard") // ng
    z = lax.axis_index("grp")
    ids = ids_ref[...]
    blk = jnp.zeros((1, n), jnp.int32)
    for k, dz in enumerate(hop_order(ng)):
        for dh in range(hi_n):
            owner = lax.rem(hi + dh, hi_n) * ng + lax.rem(z + dz, ng)
            blk = jnp.where(ids == owner, k * hi_n + dh, blk)
    onehot = lax.broadcasted_iota(jnp.int32, (nb, n), 0) == blk
    upto = lax.broadcasted_iota(jnp.int32, (n, n), 0) <= lax.broadcasted_iota(jnp.int32, (n, n), 1)
    cum = jnp.dot(
        onehot.astype(jnp.bfloat16), upto.astype(jnp.bfloat16), preferred_element_type=jnp.float32
    )
    rank = jnp.sum(jnp.where(onehot, cum, 0.0), axis=0, keepdims=True).astype(jnp.int32) - 1
    pos = blk * slots + rank
    used = cum[:, n - 1 : n].astype(jnp.int32)
    pos_ref[...] = pos
    used_ref[...] = jnp.broadcast_to(used, used_ref.shape)
    emb = emb_ref[...]
    scale = lax.rsqrt(jnp.mean(emb * emb, axis=1, keepdims=True) + 1e-06)
    units = (emb * scale).astype(jnp.bfloat16)
    units_ref[...] = units
    write_blocks(first, slots, pos, used, units, out_refs)


def pack_rest_kernel(slots, skip, pos_ref, used_ref, units_ref, *out_refs):
    units, pos, used = units_ref[...], pos_ref[...], used_ref[...]
    start, stop = skip
    write_blocks(0, slots, pos, used, units, out_refs[:start])
    write_blocks(stop, slots, pos, used, units, out_refs[start:])


def weigh_kernel(layout, row_stage, unit, slots, ng, hops, summed, carried, last, *refs):
    refs = list(refs)

    def take(count):
        got = refs[:count]
        del refs[:count]
        return got

    row_in = take(sum(c for _, _, c in row_stage))
    cols = take(sum(c for _, c in layout))
    pull_in, count_in = take(2) if summed else (None, None)
    dups_in = take(1) if carried else None
    if last:
        outs = take(len(hops))
        dups, pull, count = refs
    else:
        pull, count = refs
    width = row_in[0].shape[1]
    nrows = len(row_stage) * unit
    limit = 1.5 * width**0.5
    probe = lax.broadcasted_iota(jnp.int32, (16, width), 1) == 0
    rows = jnp.concatenate([r[...] for r in row_in] + [probe.astype(jnp.bfloat16)], axis=0)
    for at, (stage, narr) in enumerate(layout):
        part = jnp.concatenate([c[...] for c in cols[:narr]], axis=0)
        del cols[:narr]
        chunk = part.shape[0]
        scores = lax.dot_general(
            rows, part, (((1,), (1,)), ((), ())), preferred_element_type=jnp.float32
        )
        keep = jnp.broadcast_to(scores[nrows : nrows + 1, :] < limit, (nrows, chunk))
        if any(s == stage for s, _, _ in row_stage):
            col = lax.broadcasted_iota(jnp.int32, (unit, chunk), 1)
            row = lax.broadcasted_iota(jnp.int32, (unit, chunk), 0)
            off = [col != (row + h * unit if s == stage else -1) for s, h, _ in row_stage]
            keep = keep & jnp.concatenate(off, axis=0)
        weight = jnp.where(keep, jnp.exp(scores[:nrows] * (64.0 / width)), 0.0)
        add_count = jnp.broadcast_to(jnp.sum(weight, axis=1, keepdims=True), count.shape)
        add_pull = jnp.dot(weight.astype(jnp.bfloat16), part, preferred_element_type=jnp.float32)
        if at:
            count[...] += add_count
            pull[...] += add_pull
        elif summed:
            count[...] = count_in[...] + add_count
            pull[...] = pull_in[...] + add_pull
        else:
            count[...] = add_count
            pull[...] = add_pull
    if not last:
        return
    dups[...] = dups_in[0][...] if carried else jnp.zeros(dups.shape, jnp.float32)
    hi_n = dups.shape[0] // ng
    hi, z = lax.axis_index("shard") // ng, lax.axis_index("grp")
    valid = rows[:nrows, 0:128].astype(jnp.float32)[:, 0:1] < limit
    for i in range(len(hops)):
        at = i * slots
        ok = valid[at : at + slots]
        cnt = count[pl.ds(at, slots), :]
        near = pull[pl.ds(at, slots), :] / (1.0 + cnt[:, 0:1])
        outs[i][...] = jnp.where(ok, near, 0.0).astype(jnp.bfloat16)
        dup = jnp.where(ok, jnp.log1p(cnt), 0.0)
        if slots < 128:
            dup = jnp.concatenate([dup, jnp.zeros((128 - slots, 128), jnp.float32)], axis=0)
        dh, dz = hops[i]
        home = lax.rem(hi + hi_n - dh, hi_n) * ng + lax.rem(z + ng - dz, ng)
        dups[pl.ds(home, 1), :] = dup.T[0:1]


def unpack_kernel(slots, which, last, hi_n, ng, pos_ref, *refs):
    refs = list(refs)
    nwhich = len(which)
    pos = pos_ref[...]
    n = pos.shape[1]

    def pick(k):
        at = lax.broadcasted_iota(jnp.int32, (slots, n), 0) + k * slots
        return (at == pos).astype(jnp.bfloat16)

    picks = jnp.concatenate([pick(k) for k in which], axis=0)
    rows = jnp.concatenate([r[...] for r in refs[:nwhich]], axis=0)
    if not last:
        (near_ref,) = refs[nwhich:]
        near_ref[...] = lax.dot_general(
            picks, rows, (((0,), (0,)), ((), ())), preferred_element_type=jnp.float32
        )
        return
    near_in, dups, near_ref, dup_ref, near, sems = refs[nwhich:]
    step = n // 4
    copies = []
    for i in range(4):
        at = pl.ds(i * step, step)
        near[at, :] = near_in[at, :] + lax.dot_general(
            picks[:, i * step : (i + 1) * step],
            rows,
            (((0,), (0,)), ((), ())),
            preferred_element_type=jnp.float32,
        )
        copies.append(pltpu.make_async_copy(near.at[at], near_ref.at[at], sems.at[i]))
        copies[-1].start()
    hi, z = lax.axis_index("shard") // ng, lax.axis_index("grp")
    line = lax.broadcasted_iota(jnp.int32, (8, 128), 0)
    dup = jnp.zeros((8, n), jnp.float32)
    for k, (dh, dz) in enumerate((dh, dz) for dz in hop_order(ng) for dh in range(hi_n)):
        owner = lax.rem(hi + dh, hi_n) * ng + lax.rem(z + dz, ng)
        row = jnp.broadcast_to(dups[pl.ds(owner, 1), :], (8, 128))
        high = row.astype(jnp.bfloat16).astype(jnp.float32)
        two = jnp.where(line == 0, high, jnp.where(line == 1, row - high, 0.0))
        two = two.astype(jnp.bfloat16)[:, :slots]
        dup = dup + jnp.dot(two, pick(k), preferred_element_type=jnp.float32)
    dup_ref[...] = dup[0:1] + dup[1:2]
    for c in copies:
        c.wait()


def after(value, *deps):
    return lax.optimization_barrier((value,) + deps)[0]


def local(embeddings, cluster):
    n, width = embeddings.shape
    ns, ng = lax.axis_size("shard"), lax.axis_size("grp")
    hi_n = ns // ng
    nb = ns
    slots = 2 * n // ns

    def moved(f):
        return [(s * ng + z, f(s, z)) for s in range(ns) for z in range(ng)]

    def to_owner(dh, dz, sign):
        return moved(
            lambda s, z: ((s // ng + sign * dh) % hi_n * ng + s % ng) * ng + (z + sign * dz) % ng
        )

    def beside(bit):
        return moved(lambda s, z: (s ^ bit) * ng + z)

    hops = [(dh, dz) for dz in hop_order(ng) for dh in range(hi_n)]
    vmem = pl.BlockSpec(memory_space=pltpu.VMEM)
    hbm = pl.BlockSpec(memory_space=pltpu.HBM)
    ids = cluster.reshape(1, n)
    block = jax.ShapeDtypeStruct((slots, width), jnp.bfloat16)
    small = pltpu.CompilerParams(vmem_limit_bytes=16 * MIB)
    pos, used, units, *outbox = pl.pallas_call(
        functools.partial(pack_kernel, hi_n, ng, slots, hi_n),
        out_shape=[
            jax.ShapeDtypeStruct((1, n), jnp.int32),
            jax.ShapeDtypeStruct((nb, 128), jnp.int32),
            jax.ShapeDtypeStruct((n, width), jnp.bfloat16),
        ]
        + [block] * hi_n,
        in_specs=[vmem, vmem],
        out_specs=[vmem] * (hi_n + 3),
        compiler_params=small,
        name="pack",
    )(embeddings, ids)
    rest = pl.pallas_call(
        functools.partial(pack_rest_kernel, slots, (hi_n, 2 * hi_n)),
        out_shape=[block] * (nb - hi_n),
        in_specs=[vmem] * 3,
        out_specs=[vmem] * (nb - hi_n),
        compiler_params=small,
        name="pack_rest",
    )(pos, used, units)
    outbox = [*rest[:hi_n], *outbox, *rest[hi_n:]]

    per = hi_n // 2
    unit = per * slots
    nstage = ng
    own, side, other = {}, {}, {}

    def send(stage, half, *deps, cut=1):
        ks = blocks_of((stage, half))
        whole = [outbox[k] for k in ks]
        if cut > 1 and per == 1:
            pieces = [(ks[0], whole[0][i * unit // cut : (i + 1) * unit // cut]) for i in range(cut)]
        else:
            pieces = list(zip(ks, whole))
        got = []
        for k, src in pieces:
            if k:
                src = lax.ppermute(after(src, *deps) if deps else src, AXES, to_owner(*hops[k], 1))
            got.append(src)
        each = len(got) // cut
        own[stage, half] = [
            got[i] if each == 1 else jnp.concatenate(got[i : i + each], axis=0)
            for i in range(0, len(got), each)
        ]

    def across(stage, half, *deps):
        side[stage, half] = [
            lax.ppermute(after(src, *deps) if deps else src, AXES, beside(2))
            for src in own[stage, half]
        ]

    def swap(*units, deps=()):
        both = jnp.concatenate([a for t in (own, side) for u in units for a in t[u]], axis=0)
        got = lax.ppermute(after(both, *deps) if deps else both, AXES, beside(1))
        other.setdefault(units[0][0], []).append(got)

    def pieces(g):
        other[g] = [
            lax.ppermute(a, AXES, beside(1)) for t in (own, side) for h in range(2) for a in t[g, h]
        ]

    def blocks_of(unit):
        start = unit[0] * hi_n + unit[1] * per
        return range(start, start + per)

    def weigh(row_units, stages, sums=(), dups=(), last=True, deps=()):
        nrows = len(row_units) * unit
        layout, cols = [], []
        for g in stages:
            cs = own[g, 0] + own[g, 1] + side[g, 0] + side[g, 1]
            layout.append((g, len(cs)))
            cols += cs
        for g in stages:
            layout.append((None, len(other[g])))
            cols += other[g]
        total = sum(c.shape[0] for c in cols)
        row_in = [a for u in row_units for a in own[u]]
        if deps:
            row_in[0] = after(row_in[0], *deps)
        row_stage = [(g, h, len(own[g, h])) for g, h in row_units]
        ks = [k for u in row_units for k in blocks_of(u)]
        acc = [(nrows, width), (nrows, 128)]
        ins = row_in + cols + list(sums) + list(dups)
        if last:
            out_shape = [block] * len(ks) + [jax.ShapeDtypeStruct((nb, 128), jnp.float32)]
        else:
            out_shape = [jax.ShapeDtypeStruct(t, jnp.float32) for t in acc]
        return pl.pallas_call(
            functools.partial(
                weigh_kernel,
                layout,
                row_stage,
                unit,
                slots,
                ng,
                [hops[k] for k in ks],
                bool(sums),
                bool(dups),
                last,
            ),
            out_shape=out_shape,
            in_specs=[vmem] * len(ins),
            out_specs=[vmem] * len(out_shape),
            scratch_shapes=[pltpu.VMEM(t, jnp.float32) for t in acc] if last else [],
            compiler_params=pltpu.CompilerParams(vmem_limit_bytes=32 * MIB),
            cost_estimate=pl.CostEstimate(
                flops=4 * nrows * total * width if last else 0,
                bytes_accessed=2 * total * width if last else 0,
                transcendentals=nrows * total if last else 0,
            ),
            name="weigh",
        )(*ins)

    send(0, 0)
    send(1, 0)
    send(1, 1)
    send(2, 0)
    send(0, 1)
    across(0, 0, *own[1, 0])
    across(0, 1)
    across(1, 0)
    across(1, 1, *side[0, 0])
    send(2, 1, *own[1, 0])
    send(3, 0, *own[1, 1])
    send(3, 1, *own[1, 0], *own[1, 1])
    across(2, 0, *side[1, 0], *side[0, 1])
    across(2, 1, *side[1, 1])
    across(3, 0, *side[2, 0])
    across(3, 1, *side[2, 1])
    pieces(0)
    pieces(1)
    swap((2, 0), (2, 1))
    swap((3, 0))
    parts = [[(1, 0), (1, 1)], [(2, 0), (2, 1)], [(3, 0), (3, 1), (0, 1), (0, 0)]]
    stages = list(range(nstage))
    early = [0, 1]
    sums = weigh(parts[0], early, last=False, deps=side[3, 0])
    swap((3, 1), deps=sums[1:])
    result = [None] * nb
    order, dups, deps = [], (), ()
    for part in parts:
        todo = [g for g in stages if g not in early]
        *outs, dup = weigh(part, todo, sums, dups, deps=deps)
        early, sums, dups, deps = [], (), (dup,), outs[:1]
        blocks = [k for u in part for k in blocks_of(u)]
        for k, r in zip(blocks, outs):
            result[k] = r
        order += blocks
    back = [result[0]] + [None] * (nb - 1)
    for b in order:
        if b:
            back[b] = lax.ppermute(result[b], AXES, to_owner(*hops[b], -1))

    same = [
        [((h * ng + lo) * ng) + z for h in range(hi_n) for z in range(ng)] for lo in range(ng)
    ]

    def unpack(which, also, last):
        near = jax.ShapeDtypeStruct((n, width), jnp.float32)
        scratch = [pltpu.VMEM((n, width), jnp.float32), pltpu.SemaphoreType.DMA((4,))]
        return pl.pallas_call(
            functools.partial(unpack_kernel, slots, which, last, hi_n, ng),
            out_shape=[near, jax.ShapeDtypeStruct((1, n), jnp.float32)] if last else [near],
            in_specs=[vmem] * (1 + len(which) + len(also)),
            out_specs=[hbm, vmem] if last else [vmem],
            scratch_shapes=scratch if last else [],
            compiler_params=small,
            name="unpack",
        )(pos, *[back[k] for k in which], *also)

    late = [k for u in parts[2][:3] for k in blocks_of(u)]
    (near,) = unpack([b for b in range(nb) if b not in late], (), False)
    dups = lax.all_to_all(after(*dups, near), AXES, 0, 0, tiled=True, axis_index_groups=same)
    near, dup = unpack(late, (near, dups), True)
    return dup.reshape(n), near


def solution(mesh):
    return jax.shard_map(
        local,
        mesh=mesh,
        in_specs=(P(("shard", "grp"), None), P(("shard", "grp"), None)),
        out_specs=(P(("shard", "grp")), P(("shard", "grp"), None)),
        check_vma=False,
    )
```
